512 devices in a mesh: energy: 128 (over z, x, core), slab: 4 (over y).
Axes of the slice: x: 4, y: 4, z: 16, core: 2. Of those that a mesh axis runs over, the one named last changes fastest.
Arguments:
- g0e: bfloat16 [128, 8, 256, 256], P('energy', 'slab'), as said below
- hcoup: bfloat16 [8, 256, 256], P('slab'), may hold values from -0.375 to 0.375
- sigma_in: bfloat16 [128, 8, 256, 256], P('energy', 'slab'), may hold values from -4 to 4
- gph0: bfloat16 [128, 8, 256, 256], P('energy', 'slab'), as said below
- hph: bfloat16 [8, 256, 256], P('slab'), may hold values from -0.375 to 0.375
- pair_lo: int32 [128, 4], replicated, may hold values from 0 to 119
- freq_offset: int32 [128], replicated, may hold values from 1 to 8
- pair_weight: float32 [128, 4], replicated, may hold values from 0.1 to 1
- active: int32 [128], P('energy'), may hold values from 0 to 1, as said below
Outputs:
- sigma_out: bfloat16 [128, 8, 256, 256], P('energy', 'slab')
The draws below stay inside these ranges and needn't reach their ends.
Inputs may be any that keep to these rules, and one draw needn't show every extreme that they name: active holds whole numbers; the active energies of an index of energy are its first ones. `g0e`: every block is a dominant diagonal plus dense independent entries. `gph0`: every block is a dominant diagonal plus dense independent entries.
All inputs are finite; a program needn't handle non-finite values.
Results may differ from the reference program's by a relative error of at most 0.0082.
Values may be sent and summed in bfloat16 or wider, within the bound.
A program may use at most 64 MiB of HBM per device.

```python
import math
import jax
import jax.numpy as jnp
from jax import lax

B = 256
E_DEV = 1
K = 4
OMAX = 8
GROUPS = 128
ENERGIES = 128
FREQS = 128
SLABS = 8


def inverse_blocks(key, leading, spread):
    key_diag, key_off, key_rows = jax.random.split(key, 3)
    diagonal = jax.random.uniform(key_diag, leading + (B,), jnp.float32, 0.6, 1.0)
    offdiag = jax.random.normal(key_off, leading + (B, B), jnp.float32) * (0.3 / math.sqrt(B))
    row_scale = jnp.exp(jax.random.uniform(key_rows, leading + (B, 1), jnp.float32, -spread, spread))
    return (offdiag + diagonal[..., None] * jnp.eye(B, dtype=jnp.float32)) * row_scale


def draw_g0e(key, part):
    key = jax.random.fold_in(key, 11)
    blocks = inverse_blocks(key, (ENERGIES, SLABS), 0.0)
    return blocks.astype(jnp.bfloat16)


def draw_gph0(key, part):
    key = jax.random.fold_in(key, 12)
    blocks = inverse_blocks(key, (FREQS, SLABS), 0.0)
    return blocks.astype(jnp.bfloat16)


def draw_active(key, part):
    key = jax.random.fold_in(key, 13)
    key_counts, key_spot = jax.random.split(key)
    counts = jax.random.randint(key_counts, (GROUPS,), 0, E_DEV + 1)
    chosen = jax.random.randint(key_spot, (), 0, GROUPS)
    counts = counts.at[chosen].set(E_DEV)
    counts = counts.at[(chosen + 1) % GROUPS].set(0)
    return counts.astype(jnp.int32)


def place_ends(drawn, stream_key, low, top_value):
    index_at = [jax.random.randint(jax.random.fold_in(stream_key, axis), (), 0, length) for axis, length in enumerate(drawn.shape)]
    widest = drawn.shape.index(max(drawn.shape))
    beside = index_at[:widest] + [(index_at[widest] + 1) % drawn.shape[widest]] + index_at[widest + 1:]
    return drawn.at[tuple(index_at)].set(low).at[tuple(beside)].set(top_value)


def levels(own_key, dims, cuts, least, largest):
    factor_of, own = 1.0, jax.random.fold_in(own_key, 6)
    for axis_at, blocks in cuts:
        heights = jnp.exp(jax.random.uniform(jax.random.fold_in(own, axis_at), (blocks,), jnp.float32, least / len(cuts), largest / len(cuts)))
        factor_of = factor_of * jnp.repeat(heights, dims[axis_at] // blocks).reshape([-1 if axis == axis_at else 1 for axis in range(len(dims))])
    return factor_of


def scatter_about(rng, shape, scale, most, cuts=(), kind=jnp.bfloat16):
    factor_of = levels(rng, shape, cuts, -0.22, 0.18) if cuts else 1.0
    drawn = jax.random.normal(rng, shape, jnp.float32) * scale * factor_of
    return jnp.minimum(jnp.maximum(drawn, -most), most).astype(kind)


def setup_inputs(seed: int = 0) -> dict:
    key_list = jax.random.split(jax.random.key(seed), 10)
    g0e = draw_g0e(jax.random.fold_in(key_list[9], 71), 0)
    hcoup = scatter_about(key_list[1], (SLABS, B, B), B ** -0.5, 0.375, ((0, 4),))
    sigma_in = scatter_about(key_list[2], (ENERGIES, SLABS, B, B), 0.5, 4.0, ((0, 128), (1, 4)))
    gph0 = draw_gph0(jax.random.fold_in(key_list[9], 71), 0)
    hph = scatter_about(key_list[4], (SLABS, B, B), B ** -0.5, 0.375, ((0, 4),))
    pair_lo = place_ends(jax.random.randint(key_list[5], (FREQS, K), 0, ENERGIES - OMAX), jax.random.fold_in(key_list[5], 1), 0, (ENERGIES - OMAX) - 1).astype(jnp.int32)
    freq_offset = place_ends(jax.random.randint(key_list[6], (FREQS,), 1, OMAX + 1), jax.random.fold_in(key_list[6], 1), 1, OMAX).astype(jnp.int32)
    pair_weight = jnp.clip(jnp.exp(jax.random.uniform(key_list[7], (FREQS, K), jnp.float32, math.log(0.1), math.log(1.0))), 0.1, 1.0)
    active = draw_active(jax.random.fold_in(key_list[9], 71), 0)
    return {"g0e": g0e, "hcoup": hcoup, "sigma_in": sigma_in, "gph0": gph0, "hph": hph, "pair_lo": pair_lo, "freq_offset": freq_offset, "pair_weight": pair_weight, "active": active}


precise = lax.Precision.HIGHEST


def sandwich(outer, inner):
    left = jnp.einsum('nij,njk->nik', outer, inner, precision=precise)
    return jnp.einsum('nik,nlk->nil', left, outer, precision=precise)


def recursion(inverse, coupling, source):
    batch = inverse.shape[0]

    def advance(state, slab_idx):
        inv_slab = lax.dynamic_index_in_dim(inverse, slab_idx, 1, keepdims=False).astype(jnp.float32)
        coup_slab = lax.dynamic_index_in_dim(coupling, slab_idx, 0, keepdims=False).astype(jnp.float32)
        src_slab = lax.dynamic_index_in_dim(source, slab_idx, 1, keepdims=False).astype(jnp.float32)
        transfer = jnp.einsum('nij,jk->nik', inv_slab, coup_slab, precision=precise)
        injected = sandwich(inv_slab, src_slab)
        state = sandwich(transfer, state) + injected
        return state, state

    init = jnp.zeros((batch, B, B), jnp.float32)
    _, states = lax.scan(advance, init, jnp.arange(SLABS, dtype=jnp.int32))
    return jnp.swapaxes(states, 0, 1)


def reference(g0e, hcoup, sigma_in, gph0, hph, pair_lo, freq_offset, pair_weight, active):
    energy_idx = jnp.arange(ENERGIES, dtype=jnp.int32)
    active_mask = (energy_idx % E_DEV < jnp.repeat(active, E_DEV)).astype(jnp.float32)
    electron_green = recursion(g0e, hcoup, sigma_in) * active_mask[:, None, None, None]
    green_sent = electron_green.astype(jnp.bfloat16)
    top_idx = (pair_lo + freq_offset[:, None]).astype(jnp.int32)

    def polar_one(freq):
        bottom = green_sent[pair_lo[freq]].astype(jnp.float32)
        upper_blocks = green_sent[top_idx[freq]].astype(jnp.float32)
        return jnp.sum(pair_weight[freq][:, None, None, None] * bottom * upper_blocks, axis=0)

    polarization = lax.map(polar_one, jnp.arange(FREQS, dtype=jnp.int32)).astype(jnp.bfloat16)
    phonon_green = recursion(gph0, hph, polarization)
    phonon_sent = phonon_green.astype(jnp.bfloat16)

    def scatter_one(total, freq):
        phonon_block = phonon_sent[freq].astype(jnp.float32)
        weights = pair_weight[freq][:, None, None, None]
        bottom = green_sent[pair_lo[freq]].astype(jnp.float32)
        upper_blocks = green_sent[top_idx[freq]].astype(jnp.float32)
        total = total.at[pair_lo[freq]].add(weights * phonon_block[None] * upper_blocks)
        total = total.at[top_idx[freq]].add(weights * phonon_block[None] * bottom)
        return total, None

    start = jnp.zeros((ENERGIES, SLABS, B, B), jnp.float32)
    sigma_total, _ = lax.scan(scatter_one, start, jnp.arange(FREQS, dtype=jnp.int32))
    return sigma_total.astype(jnp.bfloat16)
```

```python
import functools

import jax
import jax.numpy as jnp
from jax import lax
from jax.experimental import pallas as pl
from jax.experimental.pallas import tpu as pltpu
from jax.sharding import PartitionSpec as P

MESH = pl.DeviceIdType.MESH
F32 = jnp.float32
BF16 = jnp.bfloat16
NQ = 8


def dot(a, b, dims=((1,), (0,))):
    return lax.dot_general(a, b, (dims, ((), ())), preferred_element_type=F32)


def dot_t(a, b):
    return dot(a, b, ((1,), (1,)))


def split(value):
    high = value.astype(BF16)
    return high, (value - high.astype(F32)).astype(BF16)


def left_split(parts, right, product=dot):
    return product(parts[0], right) + product(parts[1], right)


def both_split(left, right, product=dot):
    return product(left[0], right[0]) + (product(left[0], right[1]) + product(left[1], right[0]))


def ones_where(condition, dtype=BF16):
    return jnp.where(condition, jnp.ones(condition.shape, F32), jnp.zeros(condition.shape, F32)).astype(dtype)


def kernel(
    nz, ny, order, pairs,
    g0e, hcoup, sigma_in, gph0, hph, pair_lo, freq_offset, pair_weight, active,
    out,
    state_out, state_in, zsrc, zdst, qsrc, qdst, perm, perm_t, hot, hot_t, weight_cols, lows, uppers,
    zsend, zrecv, qsend, qrecv, ysend, yrecv,
):
    energies = nz * NQ
    rz = order // nz
    rq = rz // NQ
    me = lax.axis_index("energy")
    y = lax.axis_index("slab")
    z = me // NQ
    q = me % NQ

    barrier = pltpu.get_barrier_semaphore()

    def greet_z(step, carry):
        there = ((z + step) % nz) * NQ + q
        pl.semaphore_signal(barrier, inc=1, device_id=(there, y), device_id_type=MESH)
        return carry

    def greet_q(step, carry):
        there = z * NQ + (q + step) % NQ
        pl.semaphore_signal(barrier, inc=1, device_id=(there, y), device_id_type=MESH)
        return carry

    lax.fori_loop(1, nz, greet_z, 0)
    lax.fori_loop(1, NQ, greet_q, 0)

    @pl.when(y > 0)
    def _():
        pl.semaphore_signal(barrier, inc=1, device_id=(me, y - 1), device_id_type=MESH)

    @pl.when(y < ny - 1)
    def _():
        pl.semaphore_signal(barrier, inc=1, device_id=(me, y + 1), device_id_type=MESH)

    def z_rows(place):
        return pl.ds(pl.multiple_of(place * rz, rz), rz)

    def q_rows(place):
        return pl.ds(pl.multiple_of(place * nz, nz), nz)

    def z_start(lane):
        source, target = zsrc.at[lane], zdst.at[lane]

        def send(distance):
            place = (z + distance) % nz
            pltpu.make_async_remote_copy(
                src_ref=source.at[z_rows(place)],
                dst_ref=target.at[z_rows(z)],
                send_sem=zsend.at[lane],
                recv_sem=zrecv.at[lane],
                device_id=(place * NQ + q, y),
                device_id_type=MESH,
            ).start()

        send(nz // 2)

        def both(step, carry):
            distance = nz // 2 - step
            send(distance)
            send(nz - distance)
            return carry

        lax.fori_loop(1, nz // 2, both, 0)
        target[z_rows(z)] = source[z_rows(z)]

    def z_wait(lane, sems):
        view = zdst.at[lane, pl.ds(0, order - rz)]
        pltpu.make_async_copy(view, view, sems.at[lane]).wait()

    def q_start(lane):
        source, target = qsrc.at[lane], qdst.at[lane]

        def send(step, carry):
            place = (q + step) % NQ
            pltpu.make_async_remote_copy(
                src_ref=source.at[q_rows(place)],
                dst_ref=target.at[q_rows(q)],
                send_sem=qsend.at[lane],
                recv_sem=qrecv.at[lane],
                device_id=(z * NQ + place, y),
                device_id_type=MESH,
            ).start()
            return carry

        lax.fori_loop(1, NQ, send, 0)
        target[q_rows(q)] = source[q_rows(q)]

    def q_wait(lane, sems):
        view = qdst.at[lane, pl.ds(0, energies - nz)]
        pltpu.make_async_copy(view, view, sems.at[lane]).wait()

    def y_copy(which):
        return pltpu.make_async_remote_copy(
            src_ref=state_out.at[which],
            dst_ref=state_in.at[which],
            send_sem=ysend.at[which],
            recv_sem=yrecv.at[which],
            device_id=(me, (y + 1) % ny),
            device_id_type=MESH,
        )

    def enter(which):
        @pl.when(y > 0)
        def _():
            y_copy(which).wait_recv()

        @pl.when(y == 0)
        def _():
            state_in[which] = jnp.zeros((order, order), BF16)

        return state_in[which]

    def leave(which, state):
        state_out[which] = state.astype(BF16)

        @pl.when(y < ny - 1)
        def _():
            y_copy(which).start()

    def to_q(z_lane, q_lane):
        z_wait(z_lane, zrecv)
        moved = dot(perm[...], zdst[z_lane]).astype(BF16)
        for row in range(rq):
            qsrc[q_lane, :, row * order : (row + 1) * order] = moved[row * energies : (row + 1) * energies]
        q_start(q_lane)

    def to_z(q_lane, z_lane):
        q_wait(q_lane, qrecv)
        rows = [qdst[q_lane, :, row * order : (row + 1) * order] for row in range(rq)]
        zsrc[z_lane] = dot(perm_t[...], jnp.concatenate(rows, axis=0)).astype(BF16)
        z_start(z_lane)

    transfers = [dot(g0e[0, slab], hcoup[slab]) for slab in range(2)]
    injected = [
        left_split(split(dot(g0e[0, slab], sigma_in[0, slab])), g0e[0, slab], dot_t) for slab in range(2)
    ]
    transfer_parts = [split(value) for value in transfers]
    injected_parts = split(injected[0])
    mapped = split(both_split(transfer_parts[1], transfer_parts[0]))
    carried = (
        both_split(split(both_split(transfer_parts[1], injected_parts)), transfer_parts[1], dot_t) + injected[1]
    )
    keep = jnp.where(active[0] > 0, 1.0, 0.0).astype(F32)

    neighbours = jnp.minimum(y, 1) + jnp.minimum(ny - 1 - y, 1)
    pl.semaphore_wait(barrier, (nz - 1) + (NQ - 1) + neighbours)

    entered = enter(0)
    last = both_split(split(left_split(mapped, entered)), mapped, dot_t) + carried
    leave(0, last)
    first = both_split(split(left_split(transfer_parts[0], entered)), transfer_parts[0], dot_t) + injected[0]
    zsrc[0] = (keep * first).astype(BF16)
    z_start(0)
    zsrc[1] = (keep * last).astype(BF16)
    z_start(1)

    row = lax.broadcasted_iota(jnp.int32, (order, order), 0)
    col = lax.broadcasted_iota(jnp.int32, (order, order), 1)

    def source_row(place):
        return (place % nz) * rz + rq * ((place // nz) % NQ) + place // energies

    perm[...] = ones_where(source_row(row) == col)
    perm_t[...] = ones_where(row == source_row(col))
    row = lax.broadcasted_iota(jnp.int32, (energies, energies), 0)
    col = lax.broadcasted_iota(jnp.int32, (energies, energies), 1)
    energy_of_row = ((row % nz) * NQ + row // nz).astype(F32)
    energy_of_col = ((col % nz) * NQ + col // nz).astype(F32)
    diagonal = row == col
    reorder = row == (col % nz) * NQ + col // nz

    def ordered(column):
        return jnp.sum(jnp.where(reorder, column, 0.0), axis=0, keepdims=True)

    def as_column(line):
        return jnp.sum(jnp.where(diagonal, line, 0.0), axis=1, keepdims=True)

    offsets = ordered(as_column(freq_offset[...].astype(F32)))
    for k in range(pairs):
        low = ordered(as_column(pair_lo[k : k + 1].astype(F32)))
        upper = low + offsets
        weight = as_column(ordered(as_column(pair_weight[k : k + 1])))
        hot[k] = ones_where(as_column(low) == energy_of_col)
        hot[pairs + k] = ones_where(as_column(upper) == energy_of_col)
        hot_t[k] = ones_where(low == energy_of_row)
        hot_t[pairs + k] = ones_where(upper == energy_of_row)
        weight_cols[k] = jnp.broadcast_to(weight, (energies, energies))

    ph_transfers = [split(dot(gph0[0, slab], hph[slab])) for slab in range(2)]

    def polarize(slab):
        q_wait(slab, qrecv)
        total = None
        for k in range(pairs):
            bottom = dot(hot[k], qdst[slab])
            top = dot(hot[pairs + k], qdst[slab])
            weight = weight_cols[k][:, :1]
            bottom = bottom * weight
            term = bottom * top
            total = term if total is None else total + term
            lows[slab, k] = bottom
            uppers[slab, k] = top * weight
        qsrc[2 + slab] = total.astype(BF16)
        q_start(2 + slab)

    to_q(0, 0)
    polarize(0)
    to_q(1, 1)
    to_z(2, 2)
    polarize(1)
    to_z(3, 3)

    def inject(slab):
        z_wait(2 + slab, zrecv)
        return left_split(split(dot(gph0[0, slab], zdst[2 + slab])), gph0[0, slab], dot_t)

    def carry_on(transfer, state_parts):
        return both_split(split(both_split(transfer, state_parts)), transfer, dot_t)

    entered = enter(1)
    before = both_split(split(left_split(ph_transfers[0], entered)), ph_transfers[0], dot_t)
    first = before + inject(0)
    zsrc[4] = first.astype(BF16)
    z_start(4)
    before = carry_on(ph_transfers[1], split(first))
    last = before + inject(1)
    zsrc[5] = last.astype(BF16)
    z_start(5)
    leave(1, last)

    def collect(slab):
        q_wait(4 + slab, qrecv)
        phonon = qdst[4 + slab].astype(F32)
        total = None
        for k in range(pairs):
            for table, others in ((k, uppers), (pairs + k, lows)):
                high, low = split(phonon * others[slab, k])
                term = dot(hot_t[table], high) + dot(hot_t[table], low)
                total = term if total is None else total + term
        qsrc[6 + slab] = total.astype(BF16)
        q_start(6 + slab)

    to_q(4, 4)
    collect(0)
    to_q(5, 5)
    to_z(6, 6)
    collect(1)
    to_z(7, 7)
    for slab in range(2):
        z_wait(6 + slab, zrecv)
        out[0, slab] = zdst[6 + slab]

    for lane in range(8):
        z_wait(lane, zsend)
        q_wait(lane, qsend)

    @pl.when(y < ny - 1)
    def _():
        for which in range(2):
            y_copy(which).wait_send()


def per_device(g0e, hcoup, sigma_in, gph0, hph, pair_lo, freq_offset, pair_weight, active):
    groups = lax.axis_size("energy")
    ny = lax.axis_size("slab")
    nz = groups // NQ
    order = g0e.shape[2]
    pairs = pair_lo.shape[1]
    lanes = (order // nz // NQ) * order
    vmem = pl.BlockSpec(memory_space=pltpu.VMEM)
    smem = pl.BlockSpec(memory_space=pltpu.SMEM)
    return pl.pallas_call(
        functools.partial(kernel, nz, ny, order, pairs),
        out_shape=jax.ShapeDtypeStruct(g0e.shape, BF16),
        in_specs=[vmem] * 8 + [smem],
        out_specs=vmem,
        scratch_shapes=[
            pltpu.VMEM((2, order, order), BF16),
            pltpu.VMEM((2, order, order), BF16),
            pltpu.VMEM((8, order, order), BF16),
            pltpu.VMEM((8, order, order), BF16),
            pltpu.VMEM((8, groups, lanes), BF16),
            pltpu.VMEM((8, groups, lanes), BF16),
            pltpu.VMEM((order, order), BF16),
            pltpu.VMEM((order, order), BF16),
            pltpu.VMEM((2 * pairs, groups, groups), BF16),
            pltpu.VMEM((2 * pairs, groups, groups), BF16),
            pltpu.VMEM((pairs, groups, groups), F32),
            pltpu.VMEM((2, pairs, groups, lanes), F32),
            pltpu.VMEM((2, pairs, groups, lanes), F32),
            pltpu.SemaphoreType.DMA((8,)),
            pltpu.SemaphoreType.DMA((8,)),
            pltpu.SemaphoreType.DMA((8,)),
            pltpu.SemaphoreType.DMA((8,)),
            pltpu.SemaphoreType.DMA((2,)),
            pltpu.SemaphoreType.DMA((2,)),
        ],
        compiler_params=pltpu.CompilerParams(
            collective_id=0, has_side_effects=True, vmem_limit_bytes=40 * 1024 * 1024
        ),
    )(g0e, hcoup, sigma_in, gph0, hph, pair_lo.T, freq_offset.reshape(1, -1), pair_weight.T, active)


def solution(mesh):
    placed = (
        P("energy", "slab", None, None),
        P("slab", None, None),
        P("energy", "slab", None, None),
        P("energy", "slab", None, None),
        P("slab", None, None),
        P(),
        P(),
        P(),
        P("energy"),
    )
    return jax.shard_map(
        per_device,
        mesh=mesh,
        in_specs=placed,
        out_specs=P("energy", "slab", None, None),
        check_vma=False,
    )
```

```python
import functools

import jax
import jax.numpy as jnp
from jax import lax
from jax.experimental import pallas as pl
from jax.experimental.pallas import tpu as pltpu
from jax.sharding import PartitionSpec as P

MESH = pl.DeviceIdType.MESH
F32 = jnp.float32
BF16 = jnp.bfloat16
TILE = (8, 128)


def dot(a, b, dims=((1,), (0,))):
    return lax.dot_general(a, b, (dims, ((), ())), preferred_element_type=F32)


def dot_t(a, b):
    return dot(a, b, ((1,), (1,)))


def split(value):
    high = value.astype(BF16)
    return high, (value - high.astype(F32)).astype(BF16)


def left_split(parts, right, product=dot):
    return product(parts[0], right) + product(parts[1], right)


def both_split(left, right, product=dot):
    return product(left[0], right[0]) + (product(left[0], right[1]) + product(left[1], right[0]))


def ones_where(condition, dtype=BF16):
    return jnp.where(condition, jnp.ones(condition.shape, F32), jnp.zeros(condition.shape, F32)).astype(dtype)


def kernel(
    nx, nz, ny, order, pairs,
    g0e_in, hcoup_in, sigma_source, gph0_in, hph_in, pair_lo_in, freq_offset_in, pair_weight_in, active_in,
    out,
    g0e, hcoup, sigma_in, gph0, hph, pair_lo, freq_offset, pair_weight, active,
    state_out, state_in, green_tiles, green_rows, pol_rows, pol_tiles, phonon_tiles, phonon_rows, sigma_rows, sigma_tiles,
    wide, entries, hot, hot_t, weight_cols, partners,
    insem, tsend, trecv, rsend, rrecv, ysend, yrecv,
):
    chips = nx * nz
    energies = 2 * chips
    rows, lanes = TILE
    bands = order // rows
    me = lax.axis_index("energy")
    y = lax.axis_index("slab")
    chip = me // 2
    core = me % 2
    z = chip // nx
    x = chip % nx

    inputs = [
        pltpu.make_async_copy(source, target, insem.at[index])
        for index, (source, target) in enumerate(
            [
                (g0e_in, g0e),
                (hcoup_in, hcoup),
                (sigma_source, sigma_in),
                (gph0_in, gph0),
                (hph_in, hph),
                (pair_lo_in, pair_lo),
                (freq_offset_in, freq_offset),
                (pair_weight_in, pair_weight),
                (active_in, active),
            ]
        )
    ]
    for copy in inputs:
        copy.start()

    barrier = pltpu.get_barrier_semaphore()

    def greet(step, carry):
        there = (me + step) % energies
        pl.semaphore_signal(barrier, inc=1, device_id=(there, y), device_id_type=MESH)
        return carry

    lax.fori_loop(1, energies, greet, 0)

    @pl.when(y > 0)
    def _():
        pl.semaphore_signal(barrier, inc=1, device_id=(me, y - 1), device_id_type=MESH)

    @pl.when(y < ny - 1)
    def _():
        pl.semaphore_signal(barrier, inc=1, device_id=(me, y + 1), device_id_type=MESH)

    def other_chips(send):
        def at_distance(distance):
            for beside in range(nx):
                send(((z + distance) % nz) * nx + (x + beside) % nx)

        at_distance(nz // 2)

        def both(step, carry):
            distance = nz // 2 - step
            for beside in range(nx):
                send(((z + distance) % nz) * nx + (x + beside) % nx)
                send(((z + nz - distance) % nz) * nx + (x + beside) % nx)
            return carry

        lax.fori_loop(1, nz // 2, both, 0)
        for beside in range(1, nx):
            send(z * nx + (x + beside) % nx)

    def tiles_start(stage, slab, source, target):
        def copy(there):
            return pltpu.make_async_remote_copy(
                src_ref=source.at[slab, there],
                dst_ref=target.at[me],
                send_sem=tsend.at[stage],
                recv_sem=trecv.at[stage],
                device_id=(2 * there + slab, y),
                device_id_type=MESH,
            )

        other_chips(lambda there: copy(there).start())

        @pl.when(core == slab)
        def _():
            pltpu.make_async_copy(source.at[slab, chip], target.at[me], trecv.at[stage]).start()

        @pl.when(core != slab)
        def _():
            copy(chip).start()

    def rows_start(stage, source, target):
        def copy(there):
            return pltpu.make_async_remote_copy(
                src_ref=source.at[there],
                dst_ref=target.at[core, chip],
                send_sem=rsend.at[stage],
                recv_sem=rrecv.at[stage, core],
                device_id=(there, y),
                device_id_type=MESH,
            )

        def both_cores(there):
            copy(2 * there + core).start()
            copy(2 * there + 1 - core).start()

        other_chips(both_cores)
        copy(2 * chip + 1 - core).start()
        pltpu.make_async_copy(source.at[me], target.at[core, chip], rrecv.at[stage, core]).start()

    def wait_bytes(view, sem):
        pltpu.make_async_copy(view, view, sem).wait()

    def y_copy(which):
        return pltpu.make_async_remote_copy(
            src_ref=state_out.at[which],
            dst_ref=state_in.at[which],
            send_sem=ysend.at[which],
            recv_sem=yrecv.at[which],
            device_id=(me, (y + 1) % ny),
            device_id_type=MESH,
        )

    def enter(which):
        @pl.when(y > 0)
        def _():
            y_copy(which).wait_recv()

        @pl.when(y == 0)
        def _():
            state_in[which] = jnp.zeros((order, order), BF16)

        return state_in[which]

    def leave(which, state):
        state_out[which] = state.astype(BF16)

        @pl.when(y < ny - 1)
        def _():
            y_copy(which).start()

    def to_tiles(value, target):
        for side in range(order // lanes):
            half = value[:, side * lanes : (side + 1) * lanes].reshape(bands, rows, lanes)
            target[side * bands : (side + 1) * bands] = half.astype(BF16)

    def from_tiles(source):
        halves = [
            source[side * bands : (side + 1) * bands].astype(F32).reshape(order, lanes) for side in range(order // lanes)
        ]
        return jnp.concatenate(halves, axis=1).astype(BF16)

    def spread(source):
        wide[...] = source[...].astype(F32).reshape(energies * rows, lanes)

    def line(row):
        return wide[pl.ds(row, energies, stride=rows), :]

    def gather_back(target):
        target[...] = wide[...].reshape(energies, rows, lanes).astype(BF16)

    for copy in inputs[:3]:
        copy.wait()
    transfers = [dot(g0e[0, slab], hcoup[slab]) for slab in range(2)]
    injected = [
        left_split(split(dot(g0e[0, slab], sigma_in[0, slab])), g0e[0, slab], dot_t) for slab in range(2)
    ]
    transfer_parts = [split(value) for value in transfers]
    injected_parts = split(injected[0])
    mapped = split(both_split(transfer_parts[1], transfer_parts[0]))
    carried = (
        both_split(split(both_split(transfer_parts[1], injected_parts)), transfer_parts[1], dot_t) + injected[1]
    )
    for copy in inputs[3:]:
        copy.wait()
    keep = jnp.where(active[0] > 0, 1.0, 0.0).astype(F32)

    pl.semaphore_wait(barrier, (energies - 1) + jnp.minimum(y, 1) + jnp.minimum(ny - 1 - y, 1))

    entered = enter(0)
    last = both_split(split(left_split(mapped, entered)), mapped, dot_t) + carried
    leave(0, last)
    first = both_split(split(left_split(transfer_parts[0], entered)), transfer_parts[0], dot_t) + injected[0]
    to_tiles(keep * first, green_tiles.at[0])
    tiles_start(0, 0, green_tiles, green_rows)
    to_tiles(keep * last, green_tiles.at[1])
    tiles_start(0, 1, green_tiles, green_rows)

    row = lax.broadcasted_iota(jnp.int32, (energies, energies), 0)
    col = lax.broadcasted_iota(jnp.int32, (energies, energies), 1)
    diagonal = row == col
    of_row = row.astype(F32)
    of_col = col.astype(F32)

    def as_column(values):
        return jnp.sum(jnp.where(diagonal, values, 0.0), axis=1, keepdims=True)

    offsets = freq_offset[...].astype(F32)
    for k in range(pairs):
        low = pair_lo[k : k + 1].astype(F32)
        upper = low + offsets
        hot[k] = ones_where(as_column(low) == of_col)
        hot[pairs + k] = ones_where(as_column(upper) == of_col)
        hot_t[k, :, :energies] = ones_where(low == of_row)
        hot_t[k, :, energies:] = ones_where(upper == of_row)
        weight_cols[k] = jnp.broadcast_to(as_column(pair_weight[k : k + 1]), (energies, energies))

    ph_transfers = [split(dot(gph0[0, slab], hph[slab])) for slab in range(2)]
    ph_mapped = split(both_split(ph_transfers[1], ph_transfers[0]))

    wait_bytes(green_rows, trecv.at[0])
    spread(green_rows)
    for entry in range(rows):
        entries[:, entry * lanes : (entry + 1) * lanes] = line(entry).astype(BF16)
    step = 2 * lanes
    for start in range(0, rows * lanes, step):
        part = entries[:, start : start + step]
        total = None
        for k in range(pairs):
            weight = weight_cols[k][:, :1]
            term = weight * dot(hot[k], part) * dot(hot[pairs + k], part)
            total = term if total is None else total + term
        for entry in range(2):
            wide[pl.ds(start // lanes + entry, energies, stride=rows), :] = total[:, entry * lanes : (entry + 1) * lanes]
    gather_back(pol_rows)
    rows_start(0, pol_rows, pol_tiles)

    for start in range(0, rows * lanes, step):
        part = entries[:, start : start + step]
        for k in range(pairs):
            weight = weight_cols[k][:, :1]
            partners[k, :energies, start : start + step] = weight * dot(hot[pairs + k], part)
            partners[k, energies:, start : start + step] = weight * dot(hot[k], part)

    def inject(slab):
        wait_bytes(pol_tiles.at[slab], rrecv.at[0, slab])
        return left_split(split(dot(gph0[0, slab], from_tiles(pol_tiles.at[slab]))), gph0[0, slab], dot_t)

    ph_injected = inject(0)
    ph_carried = both_split(split(both_split(ph_transfers[1], split(ph_injected))), ph_transfers[1], dot_t) + inject(1)
    entered = enter(1)
    last = both_split(split(left_split(ph_mapped, entered)), ph_mapped, dot_t) + ph_carried
    leave(1, last)
    first = both_split(split(left_split(ph_transfers[0], entered)), ph_transfers[0], dot_t) + ph_injected
    to_tiles(first, phonon_tiles.at[0])
    tiles_start(1, 0, phonon_tiles, phonon_rows)
    to_tiles(last, phonon_tiles.at[1])
    tiles_start(1, 1, phonon_tiles, phonon_rows)

    wait_bytes(phonon_rows, trecv.at[1])
    spread(phonon_rows)
    for start in range(0, rows * lanes, step):
        phonon = jnp.concatenate([line(start // lanes + entry) for entry in range(2)], axis=1)
        total = None
        for k in range(pairs):
            terms = [phonon * partners[k, side * energies : (side + 1) * energies, start : start + step] for side in range(2)]
            high, low = split(jnp.concatenate(terms, axis=0))
            term = dot(hot_t[k], high) + dot(hot_t[k], low)
            total = term if total is None else total + term
        for entry in range(2):
            wide[pl.ds(start // lanes + entry, energies, stride=rows), :] = total[:, entry * lanes : (entry + 1) * lanes]
    gather_back(sigma_rows)
    rows_start(1, sigma_rows, sigma_tiles)
    for slab in range(2):
        wait_bytes(sigma_tiles.at[slab], rrecv.at[1, slab])
        out[0, slab] = from_tiles(sigma_tiles.at[slab])

    for stage in range(2):
        wait_bytes(green_rows.at[pl.ds(0, energies - 1)], tsend.at[stage])
        wait_bytes(green_rows.at[pl.ds(0, energies - 1)], rsend.at[stage])

    @pl.when(y < ny - 1)
    def _():
        for which in range(2):
            y_copy(which).wait_send()


def per_device(nx, nz, g0e, hcoup, sigma_in, gph0, hph, pair_lo, freq_offset, pair_weight, active):
    energies = lax.axis_size("energy")
    ny = lax.axis_size("slab")
    order = g0e.shape[2]
    pairs = pair_lo.shape[1]
    rows, lanes = TILE
    operands = (g0e, hcoup, sigma_in, gph0, hph, pair_lo.T, freq_offset.reshape(1, -1), pair_weight.T, active)
    tiles = pltpu.VMEM((2, energies // 2, rows, lanes), BF16)
    lines = pltpu.VMEM((energies, rows, lanes), BF16)
    blocks = pltpu.VMEM((2, order, order), BF16)
    return pl.pallas_call(
        functools.partial(kernel, nx, nz, ny, order, pairs),
        out_shape=jax.ShapeDtypeStruct(g0e.shape, BF16),
        in_specs=[pl.BlockSpec(memory_space=pl.ANY)] * len(operands),
        out_specs=pl.BlockSpec(memory_space=pltpu.VMEM),
        scratch_shapes=[pltpu.VMEM(operand.shape, operand.dtype) for operand in operands[:-1]]
        + [
            pltpu.SMEM(active.shape, active.dtype),
            blocks,
            blocks,
            tiles,
            lines,
            lines,
            tiles,
            tiles,
            lines,
            lines,
            tiles,
            pltpu.VMEM((energies * rows, lanes), F32),
            pltpu.VMEM((energies, rows * lanes), BF16),
            pltpu.VMEM((2 * pairs, energies, energies), BF16),
            pltpu.VMEM((pairs, energies, 2 * energies), BF16),
            pltpu.VMEM((pairs, energies, energies), F32),
            pltpu.VMEM((pairs, 2 * energies, rows * lanes), F32),
            pltpu.SemaphoreType.DMA((len(operands),)),
            pltpu.SemaphoreType.DMA((2,)),
            pltpu.SemaphoreType.DMA((2,)),
            pltpu.SemaphoreType.DMA((2,)),
            pltpu.SemaphoreType.DMA((2, 2)),
            pltpu.SemaphoreType.DMA((2,)),
            pltpu.SemaphoreType.DMA((2,)),
        ],
        compiler_params=pltpu.CompilerParams(
            collective_id=0, has_side_effects=True, vmem_limit_bytes=56 * 1024 * 1024
        ),
    )(*operands)


def solution(mesh):
    placed = (
        P("energy", "slab", None, None),
        P("slab", None, None),
        P("energy", "slab", None, None),
        P("energy", "slab", None, None),
        P("slab", None, None),
        P(),
        P(),
        P(),
        P("energy"),
    )
    return jax.shard_map(
        functools.partial(per_device, 4, mesh.shape["energy"] // 8),
        mesh=mesh,
        in_specs=placed,
        out_specs=P("energy", "slab", None, None),
        check_vma=False,
    )
```

```python
import functools

import jax
import jax.numpy as jnp
from jax import lax
from jax.experimental import pallas as pl
from jax.experimental.pallas import tpu as pltpu
from jax.sharding import PartitionSpec as P

MESH = pl.DeviceIdType.MESH
F32 = jnp.float32
BF16 = jnp.bfloat16
TILE = (8, 128)


def dot(a, b, dims=((1,), (0,))):
    return lax.dot_general(a, b, (dims, ((), ())), preferred_element_type=F32)


def dot_t(a, b):
    return dot(a, b, ((1,), (1,)))


def split(value):
    high = value.astype(BF16)
    return high, (value - high.astype(F32)).astype(BF16)


def left_split(parts, right, product=dot):
    return product(parts[0], right) + product(parts[1], right)


def both_split(left, right, product=dot):
    return product(left[0], right[0]) + (product(left[0], right[1]) + product(left[1], right[0]))


def ones_where(condition, dtype=BF16):
    return jnp.where(condition, jnp.ones(condition.shape, F32), jnp.zeros(condition.shape, F32)).astype(dtype)


def kernel(
    nx, nz, ny, order, pairs,
    g0e_in, hcoup_in, sigma_source, gph0_in, hph_in, pair_lo_in, freq_offset_in, pair_weight_in, active_in,
    sigma_tiles,
    g0e, hcoup, sigma_in, gph0, hph, pair_lo, freq_offset, pair_weight, active,
    state_out, state_in, held, lefts, green_tiles, green_rows, pol_rows, pol_tiles, phonon_tiles, phonon_rows, sigma_rows,
    wide, entries, hot, hot_t, weight_cols, partners,
    insem, tsend, trecv, rsend, rrecv, ysend, yrecv,
):
    chips = nx * nz
    energies = 2 * chips
    rows, lanes = TILE
    bands, sides = order // rows, order // lanes
    me = lax.axis_index("energy")
    y = lax.axis_index("slab")
    chip = me // 2
    core = me % 2
    z = chip // nx
    x = chip % nx

    inputs = [
        pltpu.make_async_copy(source, target, insem.at[index])
        for index, (source, target) in enumerate(
            [
                (g0e_in, g0e),
                (hcoup_in, hcoup),
                (sigma_source, sigma_in),
                (gph0_in, gph0),
                (hph_in, hph),
                (pair_lo_in, pair_lo),
                (freq_offset_in, freq_offset),
                (pair_weight_in, pair_weight),
                (active_in, active),
            ]
        )
    ]
    for copy in inputs:
        copy.start()

    barrier = pltpu.get_barrier_semaphore()

    def greet(step, carry):
        there = (me + step) % energies
        pl.semaphore_signal(barrier, inc=1, device_id=(there, y), device_id_type=MESH)
        return carry

    lax.fori_loop(1, energies, greet, 0, unroll=True)

    @pl.when(y > 0)
    def _():
        pl.semaphore_signal(barrier, inc=1, device_id=(me, y - 1), device_id_type=MESH)

    @pl.when(y < ny - 1)
    def _():
        pl.semaphore_signal(barrier, inc=1, device_id=(me, y + 1), device_id_type=MESH)

    def other_chips(send):
        def at_distance(distance):
            for beside in range(nx):
                send(((z + distance) % nz) * nx + (x + beside) % nx)

        at_distance(nz // 2)

        def both(step, carry):
            distance = nz // 2 - step
            for beside in range(nx):
                send(((z + distance) % nz) * nx + (x + beside) % nx)
                send(((z + nz - distance) % nz) * nx + (x + beside) % nx)
            return carry

        lax.fori_loop(1, nz // 2, both, 0)
        for beside in range(1, nx):
            send(z * nx + (x + beside) % nx)

    def to_first_chips(send):
        alone = 4

        def at(step, carry):
            turn = step - alone
            shared = jnp.where(turn % 2 == 0, nz // 2 + turn // 2, alone + turn // 2)
            place = jnp.where(jnp.logical_or(step < alone, step >= nz - alone), step, shared)
            for beside in range(nx):
                there = place * nx + (x + beside) % nx
                pl.when(there != chip)(functools.partial(send, there))
            return carry

        lax.fori_loop(0, nz, at, 0)

    def tiles_start(stage, slab, source, target):
        def copy(there):
            return pltpu.make_async_remote_copy(
                src_ref=source.at[slab, there // sides, there % sides],
                dst_ref=target.at[me],
                send_sem=tsend.at[stage, slab],
                recv_sem=trecv.at[stage],
                device_id=(2 * there + slab, y),
                device_id_type=MESH,
            )

        other_chips(lambda there: copy(there).start())

        @pl.when(core == slab)
        def _():
            pltpu.make_async_copy(source.at[slab, chip // sides, chip % sides], target.at[me], trecv.at[stage]).start()

        @pl.when(core != slab)
        def _():
            copy(chip).start()

    def tiles_sent(stage, slab):
        wait_bytes(green_rows.at[pl.ds(0, chips - 1)], tsend.at[stage, slab])

        @pl.when(core != slab)
        def _():
            wait_bytes(green_rows.at[0], tsend.at[stage, slab])

    def rows_start(stage, source, target):
        def copy(there):
            return pltpu.make_async_remote_copy(
                src_ref=source.at[there],
                dst_ref=target.at[core, chip // sides, chip % sides],
                send_sem=rsend.at[stage],
                recv_sem=rrecv.at[stage, core],
                device_id=(there, y),
                device_id_type=MESH,
            )

        def both_cores(there):
            copy(2 * there + core).start()
            copy(2 * there + 1 - core).start()

        (to_first_chips if stage else other_chips)(both_cores)
        copy(2 * chip + 1 - core).start()
        pltpu.make_async_copy(source.at[me], target.at[core, chip // sides, chip % sides], rrecv.at[stage, core]).start()

    def wait_bytes(view, sem):
        pltpu.make_async_copy(view, view, sem).wait()

    def y_copy(which, half):
        return pltpu.make_async_remote_copy(
            src_ref=state_out.at[which, half],
            dst_ref=state_in.at[which, half],
            send_sem=ysend.at[which, half],
            recv_sem=yrecv.at[which, half],
            device_id=(me, (y + 1) % ny),
            device_id_type=MESH,
        )

    def pass_on(which, half, value):
        held[1, half] = value
        state_out[which, half] = value.astype(BF16)

        @pl.when(y < ny - 1)
        def _():
            y_copy(which, half).start()

    def half_rows(value, half):
        return value[half * (order // 2) : (half + 1) * (order // 2)]

    def chain(which, scale, composed, carried, transfer, injected, source, target):
        @pl.when(y == 0)
        def _():
            for half in range(2):
                pass_on(which, half, half_rows(carried, half))
                held[0, half] = half_rows(injected, half)

        def applied(parts, half):
            return left_split([part[:, half * (order // 2) : (half + 1) * (order // 2)] for part in parts], state_in[which, half])

        def later():
            for half in range(2):
                left = [half_rows(lefts[part], half) for part in range(2)]
                pass_on(which, half, both_split(left, composed, dot_t) + half_rows(carried, half))

        @pl.when(y > 0)
        def _():
            y_copy(which, 0).wait_recv()
            through, into = applied(composed, 0), applied(transfer, 0)
            y_copy(which, 1).wait_recv()
            lefts[0], lefts[1] = split(through + applied(composed, 1))
            pl.when(y < ny - 1)(later)
            first = both_split(split(into + applied(transfer, 1)), transfer, dot_t) + injected
            for half in range(2):
                held[0, half] = half_rows(first, half)

        def go(slab):
            if slab:
                pl.when(y == ny - 1)(later)
                tiles_sent(which, 0)
            elif which:

                @pl.when(y < ny - 1)
                def _():
                    for half in range(2):
                        y_copy(which, half).wait_send()

            value = jnp.concatenate([held[slab, 0], held[slab, 1]], axis=0)
            to_tiles(value if scale is None else scale * value, source.at[slab])
            tiles_start(which, slab, source, target)

        go(0)
        return lambda: go(1)

    def to_tiles(value, target):
        for side in range(sides):
            half = value[:, side * lanes : (side + 1) * lanes].reshape(bands, rows, lanes)
            target[:, side] = half.astype(BF16)

    def from_tiles(source):
        halves = [source[:, side].astype(F32).reshape(order, lanes) for side in range(sides)]
        return jnp.concatenate(halves, axis=1).astype(BF16)

    def spread(source):
        wide[...] = source[...].astype(F32).reshape(energies * rows, lanes)

    def line(row):
        return wide[pl.ds(row, energies, stride=rows), :]

    def gather_back(target):
        target[...] = wide[...].reshape(energies, rows, lanes).astype(BF16)

    for copy in inputs[:3]:
        copy.wait()
    transfers = [dot(g0e[0, slab], hcoup[slab]) for slab in range(2)]
    injected = [
        left_split(split(dot(g0e[0, slab], sigma_in[0, slab])), g0e[0, slab], dot_t) for slab in range(2)
    ]
    transfer_parts = [split(value) for value in transfers]
    injected_parts = split(injected[0])
    mapped = split(both_split(transfer_parts[1], transfer_parts[0]))
    carried = (
        both_split(split(both_split(transfer_parts[1], injected_parts)), transfer_parts[1], dot_t) + injected[1]
    )
    for copy in inputs[3:]:
        copy.wait()
    keep = jnp.where(active[0] > 0, 1.0, 0.0).astype(F32)

    pl.semaphore_wait(barrier, (energies - 1) + jnp.minimum(y, 1) + jnp.minimum(ny - 1 - y, 1))

    second_electrons = chain(0, keep, mapped, carried, transfer_parts[0], injected[0], green_tiles, green_rows)

    row = lax.broadcasted_iota(jnp.int32, (energies, energies), 0)
    col = lax.broadcasted_iota(jnp.int32, (energies, energies), 1)
    diagonal = row == col
    of_row = row.astype(F32)
    of_col = col.astype(F32)

    def as_column(values):
        return jnp.sum(jnp.where(diagonal, values, 0.0), axis=1, keepdims=True)

    offsets = freq_offset[...].astype(F32)
    for k in range(pairs):
        low = pair_lo[k : k + 1].astype(F32)
        upper = low + offsets
        hot[k] = ones_where(as_column(low) == of_col)
        hot[pairs + k] = ones_where(as_column(upper) == of_col)
        hot_t[k, :, :energies] = ones_where(low == of_row)
        hot_t[k, :, energies:] = ones_where(upper == of_row)
        weight_cols[k] = jnp.broadcast_to(as_column(pair_weight[k : k + 1]), (energies, energies))

    ph_transfers = [split(dot(gph0[0, slab], hph[slab])) for slab in range(2)]
    ph_mapped = split(both_split(ph_transfers[1], ph_transfers[0]))

    second_electrons()

    wait_bytes(green_rows, trecv.at[0])
    spread(green_rows)
    for entry in range(rows):
        entries[:, entry * lanes : (entry + 1) * lanes] = line(entry).astype(BF16)
    step = 2 * lanes
    for start in range(0, rows * lanes, step):
        part = entries[:, start : start + step]
        total = None
        for k in range(pairs):
            weight = weight_cols[k][:, :1]
            term = weight * dot(hot[k], part) * dot(hot[pairs + k], part)
            total = term if total is None else total + term
        for entry in range(2):
            wide[pl.ds(start // lanes + entry, energies, stride=rows), :] = total[:, entry * lanes : (entry + 1) * lanes]
    gather_back(pol_rows)
    rows_start(0, pol_rows, pol_tiles)

    for start in range(0, rows * lanes, step):
        part = entries[:, start : start + step]
        for k in range(pairs):
            weight = weight_cols[k][:, :1]
            partners[k, :energies, start : start + step] = weight * dot(hot[pairs + k], part)
            partners[k, energies:, start : start + step] = weight * dot(hot[k], part)

    def inject(slab):
        wait_bytes(pol_tiles.at[slab], rrecv.at[0, slab])
        return left_split(split(dot(gph0[0, slab], from_tiles(pol_tiles.at[slab]))), gph0[0, slab], dot_t)

    ph_injected = inject(0)
    ph_carried = both_split(split(both_split(ph_transfers[1], split(ph_injected))), ph_transfers[1], dot_t) + inject(1)
    chain(1, None, ph_mapped, ph_carried, ph_transfers[0], ph_injected, phonon_tiles, phonon_rows)()

    wait_bytes(phonon_rows, trecv.at[1])
    spread(phonon_rows)
    for start in range(0, rows * lanes, step):
        phonon = jnp.concatenate([line(start // lanes + entry) for entry in range(2)], axis=1)
        total = None
        for k in range(pairs):
            terms = [phonon * partners[k, side * energies : (side + 1) * energies, start : start + step] for side in range(2)]
            high, low = split(jnp.concatenate(terms, axis=0))
            term = dot(hot_t[k], high) + dot(hot_t[k], low)
            total = term if total is None else total + term
        for entry in range(2):
            wide[pl.ds(start // lanes + entry, energies, stride=rows), :] = total[:, entry * lanes : (entry + 1) * lanes]
    gather_back(sigma_rows)
    rows_start(1, sigma_rows, sigma_tiles)
    for slab in range(2):
        wait_bytes(sigma_tiles.at[slab], rrecv.at[1, slab])

    for stage in range(2):
        tiles_sent(stage, 1)
        wait_bytes(green_rows.at[pl.ds(0, energies - 1)], rsend.at[stage])

    @pl.when(y < ny - 1)
    def _():
        for which, half in ((0, 0), (0, 1)):
            y_copy(which, half).wait_send()


def per_device(nx, nz, g0e, hcoup, sigma_in, gph0, hph, pair_lo, freq_offset, pair_weight, active):
    energies = lax.axis_size("energy")
    ny = lax.axis_size("slab")
    order = g0e.shape[2]
    pairs = pair_lo.shape[1]
    rows, lanes = TILE
    operands = (g0e, hcoup, sigma_in, gph0, hph, pair_lo.T, freq_offset.reshape(1, -1), pair_weight.T, active)
    tiles = pltpu.VMEM((2, order // rows, order // lanes, rows, lanes), BF16)
    lines = pltpu.VMEM((energies, rows, lanes), BF16)
    blocks = pltpu.VMEM((2, 2, order // 2, order), BF16)
    result = pl.pallas_call(
        functools.partial(kernel, nx, nz, ny, order, pairs),
        out_shape=tiles,
        in_specs=[pl.BlockSpec(memory_space=pl.ANY)] * len(operands),
        out_specs=pl.BlockSpec(memory_space=pltpu.VMEM),
        scratch_shapes=[pltpu.VMEM(operand.shape, operand.dtype) for operand in operands[:-1]]
        + [
            pltpu.SMEM(active.shape, active.dtype),
            blocks,
            blocks,
            pltpu.VMEM((2, 2, order // 2, order), F32),
            pltpu.VMEM((2, order, order), BF16),
            tiles,
            lines,
            lines,
            tiles,
            tiles,
            lines,
            lines,
            pltpu.VMEM((energies * rows, lanes), F32),
            pltpu.VMEM((energies, rows * lanes), BF16),
            pltpu.VMEM((2 * pairs, energies, energies), BF16),
            pltpu.VMEM((pairs, energies, 2 * energies), BF16),
            pltpu.VMEM((pairs, energies, energies), F32),
            pltpu.VMEM((pairs, 2 * energies, rows * lanes), F32),
            pltpu.SemaphoreType.DMA((len(operands),)),
            pltpu.SemaphoreType.DMA((2, 2)),
            pltpu.SemaphoreType.DMA((2,)),
            pltpu.SemaphoreType.DMA((2,)),
            pltpu.SemaphoreType.DMA((2, 2)),
            pltpu.SemaphoreType.DMA((2, 2)),
            pltpu.SemaphoreType.DMA((2, 2)),
        ],
        compiler_params=pltpu.CompilerParams(
            collective_id=0, has_side_effects=True, vmem_limit_bytes=56 * 1024 * 1024
        ),
    )(*operands)
    bands, sides = order // rows, order // lanes
    return result.reshape(g0e.shape[:2] + (bands, sides, rows, lanes)).transpose(0, 1, 2, 4, 3, 5).reshape(g0e.shape)


def solution(mesh):
    placed = (
        P("energy", "slab", None, None),
        P("slab", None, None),
        P("energy", "slab", None, None),
        P("energy", "slab", None, None),
        P("slab", None, None),
        P(),
        P(),
        P(),
        P("energy"),
    )
    return jax.shard_map(
        functools.partial(per_device, 4, mesh.shape["energy"] // 8),
        mesh=mesh,
        in_specs=placed,
        out_specs=P("energy", "slab", None, None),
        check_vma=False,
    )
```

```python
import functools

import jax
import jax.numpy as jnp
from jax import lax
from jax.experimental import pallas as pl
from jax.experimental.pallas import tpu as pltpu
from jax.sharding import PartitionSpec as P

MESH = pl.DeviceIdType.MESH
F32 = jnp.float32
BF16 = jnp.bfloat16
TILE = (8, 128)


def dot(a, b, dims=((1,), (0,))):
    return lax.dot_general(a, b, (dims, ((), ())), preferred_element_type=F32)


def dot_t(a, b):
    return dot(a, b, ((1,), (1,)))


def split(value):
    high = value.astype(BF16)
    return high, (value - high.astype(F32)).astype(BF16)


def left_split(parts, right, product=dot):
    return product(parts[0], right) + product(parts[1], right)


def both_split(left, right, product=dot):
    return product(left[0], right[0]) + (product(left[0], right[1]) + product(left[1], right[0]))


def ones_where(condition, dtype=BF16):
    return jnp.where(condition, jnp.ones(condition.shape, F32), jnp.zeros(condition.shape, F32)).astype(dtype)


def kernel(
    nx, nz, ny, order, pairs,
    g0e_in, hcoup_in, sigma_source, gph0_in, hph_in, pair_lo_in, freq_offset_in, pair_weight_in, active_in,
    sigma_tiles,
    g0e, hcoup, sigma_in, gph0, hph, pair_lo, freq_offset, pair_weight, active,
    state_out, state_in, held, lefts, green_tiles, green_rows, pol_rows, pol_tiles, phonon_tiles, phonon_rows, sigma_rows,
    wide, entries, hot, hot_t, weight_cols, partners,
    insem, tsend, trecv, rsend, rrecv, ysend, yrecv,
):
    chips = nx * nz
    energies = 2 * chips
    rows, lanes = TILE
    bands, sides = order // rows, order // lanes
    me = lax.axis_index("energy")
    y = lax.axis_index("slab")
    chip = me // 2
    core = me % 2
    z = chip // nx
    x = chip % nx

    inputs = [
        pltpu.make_async_copy(source, target, insem.at[index])
        for index, (source, target) in enumerate(
            [
                (g0e_in, g0e),
                (hcoup_in, hcoup),
                (sigma_source, sigma_in),
                (gph0_in, gph0),
                (hph_in, hph),
                (pair_lo_in, pair_lo),
                (freq_offset_in, freq_offset),
                (pair_weight_in, pair_weight),
                (active_in, active),
            ]
        )
    ]
    for copy in inputs:
        copy.start()

    barrier = pltpu.get_barrier_semaphore()

    def greet(step, carry):
        there = (me + step) % energies
        pl.semaphore_signal(barrier, inc=1, device_id=(there, y), device_id_type=MESH)
        return carry

    @pl.when(y > 0)
    def _():
        pl.semaphore_signal(barrier, inc=1, device_id=(me, y - 1), device_id_type=MESH)

    @pl.when(y < ny - 1)
    def _():
        pl.semaphore_signal(barrier, inc=1, device_id=(me, y + 1), device_id_type=MESH)

    def greet_far(turn, carry):
        greet(energies // 2 + (turn + 1) // 2, 0)
        greet(energies // 2 - (turn + 1) // 2, 0)
        return carry

    greet(energies // 2, 0)
    lax.fori_loop(0, energies // 2 - 1, lambda turn, carry: greet_far(2 * turn + 1, carry), 0)

    def other_chips(send):
        def at_distance(distance):
            for beside in sorted(range(nx), key=lambda step: -min(step, nx - step)):
                send(((z + distance) % nz) * nx + (x + beside) % nx)

        at_distance(nz // 2)

        def both(step, carry):
            distance = nz // 2 - step
            for beside in sorted(range(nx), key=lambda step: -min(step, nx - step)):
                send(((z + distance) % nz) * nx + (x + beside) % nx)
                send(((z + nz - distance) % nz) * nx + (x + beside) % nx)
            return carry

        lax.fori_loop(1, nz // 2, both, 0)
        for beside in range(1, nx):
            send(z * nx + (x + beside) % nx)

    def to_first_chips(send):
        alone = 4

        def at(step, carry):
            turn = step - alone
            shared = jnp.where(turn % 2 == 0, nz // 2 + turn // 2, alone + turn // 2)
            place = jnp.where(jnp.logical_or(step < alone, step >= nz - alone), step, shared)
            for beside in range(nx):
                there = place * nx + (x + beside) % nx
                pl.when(there != chip)(functools.partial(send, there))
            return carry

        lax.fori_loop(0, nz, at, 0)

    def tiles_start(stage, slab, source, target):
        def copy(there):
            return pltpu.make_async_remote_copy(
                src_ref=source.at[slab, there // sides, there % sides],
                dst_ref=target.at[me],
                send_sem=tsend.at[stage, slab],
                recv_sem=trecv.at[stage],
                device_id=(2 * there + slab, y),
                device_id_type=MESH,
            )

        other_chips(lambda there: copy(there).start())

        @pl.when(core == slab)
        def _():
            pltpu.make_async_copy(source.at[slab, chip // sides, chip % sides], target.at[me], trecv.at[stage]).start()

        @pl.when(core != slab)
        def _():
            copy(chip).start()

    def tiles_sent(stage, slab):
        wait_bytes(green_rows.at[pl.ds(0, chips - 1)], tsend.at[stage, slab])

        @pl.when(core != slab)
        def _():
            wait_bytes(green_rows.at[0], tsend.at[stage, slab])

    def rows_start(stage, source, target):
        def copy(there):
            return pltpu.make_async_remote_copy(
                src_ref=source.at[there],
                dst_ref=target.at[core, chip // sides, chip % sides],
                send_sem=rsend.at[stage],
                recv_sem=rrecv.at[stage, core],
                device_id=(there, y),
                device_id_type=MESH,
            )

        def both_cores(there):
            copy(2 * there + core).start()
            copy(2 * there + 1 - core).start()

        (to_first_chips if stage else other_chips)(both_cores)
        copy(2 * chip + 1 - core).start()
        pltpu.make_async_copy(source.at[me], target.at[core, chip // sides, chip % sides], rrecv.at[stage, core]).start()

    def wait_bytes(view, sem):
        pltpu.make_async_copy(view, view, sem).wait()

    def y_copy(which, half):
        return pltpu.make_async_remote_copy(
            src_ref=state_out.at[which, half],
            dst_ref=state_in.at[which, half],
            send_sem=ysend.at[which, half],
            recv_sem=yrecv.at[which, half],
            device_id=(me, (y + 1) % ny),
            device_id_type=MESH,
        )

    def pass_on(which, half, value):
        held[1, half] = value
        state_out[which, half] = value.astype(BF16)

        @pl.when(y < ny - 1)
        def _():
            y_copy(which, half).start()

    def half_rows(value, half):
        return value[half * (order // 2) : (half + 1) * (order // 2)]

    def chain(which, scale, composed, carried, transfer, injected, source, target):
        @pl.when(y == 0)
        def _():
            for half in range(2):
                pass_on(which, half, half_rows(carried, half))
                held[0, half] = half_rows(injected, half)

        def applied(parts, half):
            return left_split([part[:, half * (order // 2) : (half + 1) * (order // 2)] for part in parts], state_in[which, half])

        def later():
            for half in range(2):
                left = [half_rows(lefts[part], half) for part in range(2)]
                pass_on(which, half, both_split(left, composed, dot_t) + half_rows(carried, half))

        @pl.when(y > 0)
        def _():
            y_copy(which, 0).wait_recv()
            through, into = applied(composed, 0), applied(transfer, 0)
            y_copy(which, 1).wait_recv()
            lefts[0], lefts[1] = split(through + applied(composed, 1))
            pl.when(y < ny - 1)(later)
            first = both_split(split(into + applied(transfer, 1)), transfer, dot_t) + injected
            for half in range(2):
                held[0, half] = half_rows(first, half)

        def go(slab):
            if slab:
                pl.when(y == ny - 1)(later)
                tiles_sent(which, 0)
            elif which:

                @pl.when(y < ny - 1)
                def _():
                    for half in range(2):
                        y_copy(which, half).wait_send()

            value = jnp.concatenate([held[slab, 0], held[slab, 1]], axis=0)
            to_tiles(value if scale is None else scale * value, source.at[slab])
            tiles_start(which, slab, source, target)

        go(0)
        return lambda: go(1)

    def to_tiles(value, target):
        for side in range(sides):
            half = value[:, side * lanes : (side + 1) * lanes].reshape(bands, rows, lanes)
            target[:, side] = half.astype(BF16)

    def from_tiles(source):
        halves = [source[:, side].astype(F32).reshape(order, lanes) for side in range(sides)]
        return jnp.concatenate(halves, axis=1).astype(BF16)

    def spread(source):
        wide[: energies * rows] = source[...].astype(F32).reshape(energies * rows, lanes)

    def line(row):
        return wide[pl.ds(row, energies, stride=rows), :]

    def gather_back(target):
        target[...] = wide[: energies * rows].reshape(energies, rows, lanes).astype(BF16)

    for copy in inputs[:3]:
        copy.wait()
    transfers = [dot(g0e[0, slab], hcoup[slab]) for slab in range(2)]
    injected = [
        left_split(split(dot(g0e[0, slab], sigma_in[0, slab])), g0e[0, slab], dot_t) for slab in range(2)
    ]
    transfer_parts = [split(value) for value in transfers]
    injected_parts = split(injected[0])
    mapped = split(both_split(transfer_parts[1], transfer_parts[0]))
    carried = (
        both_split(split(both_split(transfer_parts[1], injected_parts)), transfer_parts[1], dot_t) + injected[1]
    )
    for copy in inputs[3:]:
        copy.wait()
    keep = jnp.where(active[0] > 0, 1.0, 0.0).astype(F32)

    pl.semaphore_wait(barrier, (energies - 1) + jnp.minimum(y, 1) + jnp.minimum(ny - 1 - y, 1))

    second_electrons = chain(0, keep, mapped, carried, transfer_parts[0], injected[0], green_tiles, green_rows)

    row = lax.broadcasted_iota(jnp.int32, (energies, energies), 0)
    col = lax.broadcasted_iota(jnp.int32, (energies, energies), 1)
    diagonal = row == col
    of_row = row.astype(F32)
    of_col = col.astype(F32)

    def as_column(values):
        return jnp.sum(jnp.where(diagonal, values, 0.0), axis=1, keepdims=True)

    offsets = freq_offset[...].astype(F32)
    for k in range(pairs):
        low = pair_lo[k : k + 1].astype(F32)
        upper = low + offsets
        hot[k] = ones_where(as_column(low) == of_col)
        hot[pairs + k] = ones_where(as_column(upper) == of_col)
        hot_t[:, 2 * k * energies : (2 * k + 1) * energies] = ones_where(low == of_row)
        hot_t[:, (2 * k + 1) * energies : (2 * k + 2) * energies] = ones_where(upper == of_row)
        weight_cols[k] = jnp.broadcast_to(as_column(pair_weight[k : k + 1]), (energies, energies))

    ph_transfers = [split(dot(gph0[0, slab], hph[slab])) for slab in range(2)]
    ph_mapped = split(both_split(ph_transfers[1], ph_transfers[0]))

    second_electrons()

    wait_bytes(green_rows, trecv.at[0])
    spread(green_rows)
    for entry in range(rows):
        entries[:, entry * lanes : (entry + 1) * lanes] = line(entry).astype(BF16)
    step = 2 * lanes
    for start in range(0, rows * lanes, step):
        part = entries[:, start : start + step]
        total = None
        for k in range(pairs):
            weight = weight_cols[k][:, :1]
            term = weight * dot(hot[k], part) * dot(hot[pairs + k], part)
            total = term if total is None else total + term
        for entry in range(2):
            wide[pl.ds(start // lanes + entry, energies, stride=rows), :] = total[:, entry * lanes : (entry + 1) * lanes]
    gather_back(pol_rows)
    rows_start(0, pol_rows, pol_tiles)

    for start in range(0, rows * lanes, step):
        part = entries[:, start : start + step]
        for k in range(pairs):
            weight = weight_cols[k][:, :1]
            partners[k, :energies, start : start + step] = weight * dot(hot[pairs + k], part)
            partners[k, energies:, start : start + step] = weight * dot(hot[k], part)

    def inject(slab):
        wait_bytes(pol_tiles.at[slab], rrecv.at[0, slab])
        return left_split(split(dot(gph0[0, slab], from_tiles(pol_tiles.at[slab]))), gph0[0, slab], dot_t)

    ph_injected = inject(0)
    ph_carried = both_split(split(both_split(ph_transfers[1], split(ph_injected))), ph_transfers[1], dot_t) + inject(1)
    chain(1, None, ph_mapped, ph_carried, ph_transfers[0], ph_injected, phonon_tiles, phonon_rows)()

    wait_bytes(phonon_rows, trecv.at[1])
    spread(phonon_rows)
    for start in range(0, rows * lanes, step):
        phonon = jnp.concatenate([line(start // lanes + entry) for entry in range(2)], axis=1)
        terms = [
            (phonon * partners[k, side * energies : (side + 1) * energies, start : start + step]).astype(BF16)
            for k in range(pairs)
            for side in range(2)
        ]
        total = dot(hot_t[...], jnp.concatenate(terms, axis=0))
        for entry in range(2):
            wide[pl.ds(start // lanes + entry, energies, stride=rows), :] = total[:, entry * lanes : (entry + 1) * lanes]
    gather_back(sigma_rows)
    rows_start(1, sigma_rows, sigma_tiles)
    for slab in range(2):
        wait_bytes(sigma_tiles.at[slab], rrecv.at[1, slab])

    for stage in range(2):
        tiles_sent(stage, 1)
        wait_bytes(green_rows.at[pl.ds(0, energies - 1)], rsend.at[stage])

    @pl.when(y < ny - 1)
    def _():
        for which, half in ((0, 0), (0, 1)):
            y_copy(which, half).wait_send()


def per_device(nx, nz, g0e, hcoup, sigma_in, gph0, hph, pair_lo, freq_offset, pair_weight, active):
    energies = lax.axis_size("energy")
    ny = lax.axis_size("slab")
    order = g0e.shape[2]
    pairs = pair_lo.shape[1]
    rows, lanes = TILE
    operands = (g0e, hcoup, sigma_in, gph0, hph, pair_lo.T, freq_offset.reshape(1, -1), pair_weight.T, active)
    tiles = pltpu.VMEM((2, order // rows, order // lanes, rows, lanes), BF16)
    lines = pltpu.VMEM((energies, rows, lanes), BF16)
    blocks = pltpu.VMEM((2, 2, order // 2, order), BF16)
    result = pl.pallas_call(
        functools.partial(kernel, nx, nz, ny, order, pairs),
        out_shape=tiles,
        in_specs=[pl.BlockSpec(memory_space=pl.ANY)] * len(operands),
        out_specs=pl.BlockSpec(memory_space=pltpu.VMEM),
        scratch_shapes=[pltpu.VMEM(operand.shape, operand.dtype) for operand in operands[:-1]]
        + [
            pltpu.SMEM(active.shape, active.dtype),
            blocks,
            blocks,
            pltpu.VMEM((2, 2, order // 2, order), F32),
            pltpu.VMEM((2, order, order), BF16),
            tiles,
            lines,
            lines,
            tiles,
            tiles,
            lines,
            lines,
            pltpu.VMEM((energies * rows + rows, lanes), F32),
            pltpu.VMEM((energies, rows * lanes), BF16),
            pltpu.VMEM((2 * pairs, energies, energies), BF16),
            pltpu.VMEM((energies, 2 * pairs * energies), BF16),
            pltpu.VMEM((pairs, energies, energies), F32),
            pltpu.VMEM((pairs, 2 * energies, rows * lanes), F32),
            pltpu.SemaphoreType.DMA((len(operands),)),
            pltpu.SemaphoreType.DMA((2, 2)),
            pltpu.SemaphoreType.DMA((2,)),
            pltpu.SemaphoreType.DMA((2,)),
            pltpu.SemaphoreType.DMA((2, 2)),
            pltpu.SemaphoreType.DMA((2, 2)),
            pltpu.SemaphoreType.DMA((2, 2)),
        ],
        compiler_params=pltpu.CompilerParams(
            collective_id=0, has_side_effects=True, vmem_limit_bytes=56 * 1024 * 1024
        ),
    )(*operands)
    bands, sides = order // rows, order // lanes
    return result.reshape(g0e.shape[:2] + (bands, sides, rows, lanes)).transpose(0, 1, 2, 4, 3, 5).reshape(g0e.shape)


def solution(mesh):
    placed = (
        P("energy", "slab", None, None),
        P("slab", None, None),
        P("energy", "slab", None, None),
        P("energy", "slab", None, None),
        P("slab", None, None),
        P(),
        P(),
        P(),
        P("energy"),
    )
    return jax.shard_map(
        functools.partial(per_device, 4, mesh.shape["energy"] // 8),
        mesh=mesh,
        in_specs=placed,
        out_specs=P("energy", "slab", None, None),
        check_vma=False,
    )
```
